32 devices in a mesh: grp: 2 (over y), col: 4 (over z), row: 2 (over x), sub: 2 (over core).
Axes of the slice: x: 2, y: 2, z: 4, core: 2. Of those that a mesh axis runs over, the one named last changes fastest.
Arguments:
- counts: int32 [8, 4], P(('grp', 'row', 'sub'), 'col'), parts along dimension 0, may hold values from 1 to 12, as said below
- point_x: int32 [8, 4, 1536], P(('grp', 'row', 'sub'), 'col'), parts along dimension 0, may hold values from 0 to 511
- point_y: int32 [8, 4, 1536], P(('grp', 'row', 'sub'), 'col'), parts along dimension 0, may hold values from 0 to 255
- point_rate: float32 [8, 4, 1536], P(('grp', 'row', 'sub'), 'col'), parts along dimension 0, may hold values from 0.003125 to 0.0234375
- point_amp: float32 [8, 4, 2, 1536], P(('grp', 'row', 'sub'), 'col'), parts along dimension 0, may hold values from -2 to 2
- prop_rate: float32 [1], replicated, may hold values from 0.003125 to 0.0234375
Outputs:
- hologram: float32 [2, 2048, 2048], P(None, ('grp', 'row', 'sub'), 'col'), parts along dimension 1
The draws below stay inside these ranges and needn't reach their ends.
There are 2 independent parts, one for each index of `grp`. The reference program is written for one: setup_inputs(seed, part) draws one part's arguments, and reference() takes and returns one part's arrays. A program takes and returns all parts, laid end to end along the dimension named above; an argument that names none is the same for every part. Nothing has to cross between parts.
Inputs may be any that keep to these rules, and one draw needn't show every extreme that they name: Tile part (ty, tx) has counts[ty, tx] live blocks of 128 points; in every plane some tile part has all 12 blocks live.
All inputs are finite; a program needn't handle non-finite values.
Results may differ from the reference program's by a relative error of at most 0.0037.
Values sent between devices are 32-bit elements; how exact they have to be, the bound alone decides.
A program may use at most 64 MiB of HBM per device.

```python
import math
import jax
import jax.numpy as jnp
from jax import lax

TW = 512
TH = 256
RZ = 64
HB = 64
BP = 128
NB = 12
NTY = 4
NTX = 4
NY = 1024
NX = 2048


def draw_counts(key, part):
    key = jax.random.fold_in(key, 7)
    key_base, key_busy, key_pick = jax.random.split(key, 3)
    base_blocks = jax.random.randint(key_base, (NTY, NTX), 1, NB // 2 + 1)
    busy_flags = jax.random.randint(key_busy, (NTY, NTX), 0, 8) == 0
    blocks_live = jnp.where(busy_flags, NB, base_blocks).reshape(-1)
    chosen = jax.random.randint(key_pick, (), 0, NTY * NTX)
    blocks_live = blocks_live.at[chosen].set(NB)
    return blocks_live.reshape(NTY, NTX).astype(jnp.int32)


def touch_ends(entries, own_key, least, top_value):
    index_at = [jax.random.randint(jax.random.fold_in(own_key, axis), (), 0, length) for axis, length in enumerate(entries.shape)]
    longest = entries.shape.index(max(entries.shape))
    next_to = index_at[:longest] + [(index_at[longest] + 1) % entries.shape[longest]] + index_at[longest + 1:]
    return entries.at[tuple(index_at)].set(least).at[tuple(next_to)].set(top_value)


def levels(rng, shape, shards, least, top_value):
    def one(dim, shards_of):
        steps = jax.random.uniform(jax.random.fold_in(jax.random.fold_in(rng, 6), dim), (shards_of,), jnp.float32, least / len(shards), top_value / len(shards))
        return jnp.repeat(jnp.exp(steps), shape[dim] // shards_of).reshape((-1,) + (1,) * (len(shape) - dim - 1))

    level = one(*shards[0])
    for cut in shards[1:]:
        level = level * one(*cut)
    return level


def normal_values(stream_key, extent, width, bound, cuts=(), kind=jnp.bfloat16):
    values = jax.random.normal(stream_key, extent, jnp.float32) * width
    if len(cuts) > 0:
        values = levels(stream_key, extent, cuts, -0.22, 0.18) * values
    return jnp.clip(values, min=-bound, max=bound).astype(kind)


def setup_inputs(seed: int = 0, part: int = 0) -> dict:
    key_of = jax.random.split(jax.random.key(seed), 7)
    part_splits = jax.random.split(jax.random.fold_in(key_of[6], part), 7)
    counts = draw_counts(jax.random.fold_in(jax.random.fold_in(key_of[6], part), 71), part)
    point_x = touch_ends(jax.random.randint(part_splits[1], (NTY, NTX, NB * BP), 0, TW), jax.random.fold_in(part_splits[1], 1), 0, TW - 1).astype(jnp.int32)
    point_y = touch_ends(jax.random.randint(part_splits[2], (NTY, NTX, NB * BP), 0, TH), jax.random.fold_in(part_splits[2], 1), 0, TH - 1).astype(jnp.int32)
    point_rate = jnp.clip(jnp.exp(math.log(0.0234375) - 2.014903 * jax.random.uniform(part_splits[3], (NTY, NTX, NB * BP), jnp.float32) ** levels(part_splits[3], (NTY, NTX, NB * BP), ((0, 4), (1, 4)), -0.2, 0.2)), 0.003125, 0.0234375)
    point_amp = normal_values(part_splits[4], (NTY, NTX, 2, NB * BP), (0.6 * (TH * TW) ** 0.5 / (BP * (2 * RZ + 1) ** 2) ** 0.5), 2.0, ((0, 4), (1, 4)), jnp.float32)
    prop_rate = jnp.clip(jnp.exp(jax.random.uniform(key_of[5], (1,), jnp.float32, math.log(0.003125), math.log(0.0234375))), 0.003125, 0.0234375)
    return dict(counts=counts, point_x=point_x, point_y=point_y, point_rate=point_rate, point_amp=point_amp, prop_rate=prop_rate)


def block_field(pos_cols, pos_rows, point_rates, point_amps):
    win_cols = TW + 2 * RZ
    win_rows = TH + 2 * RZ
    col_dist = jnp.arange(win_cols, dtype=jnp.float32)[None, :] - RZ - pos_cols[:, None]
    row_dist = jnp.arange(win_rows, dtype=jnp.float32)[None, :] - RZ - pos_rows[:, None]
    phase_x = point_rates[:, None] * col_dist * col_dist
    phase_y = point_rates[:, None] * row_dist * row_dist
    inside_x = jnp.abs(col_dist) <= RZ
    inside_y = jnp.abs(row_dist) <= RZ
    wave_re = jnp.where(inside_x, jnp.cos(phase_x), 0.0)
    wave_im = jnp.where(inside_x, jnp.sin(phase_x), 0.0)
    g_re = (point_amps[0][:, None] * wave_re - point_amps[1][:, None] * wave_im).astype(jnp.bfloat16)
    g_im = (point_amps[0][:, None] * wave_im + point_amps[1][:, None] * wave_re).astype(jnp.bfloat16)
    ey_re = jnp.where(inside_y, jnp.cos(phase_y), 0.0).astype(jnp.bfloat16)
    ey_im = jnp.where(inside_y, jnp.sin(phase_y), 0.0).astype(jnp.bfloat16)
    left_stack = jnp.concatenate([jnp.concatenate([ey_re, ey_im], 1), jnp.concatenate([-ey_im, ey_re], 1)], 0)
    right_stack = jnp.concatenate([g_re, g_im], 0)
    product = lax.dot_general(left_stack.astype(jnp.float32), right_stack.astype(jnp.float32), (((0,), (0,)), ((), ())), precision=lax.Precision.HIGHEST, preferred_element_type=jnp.float32)
    return product.reshape(2, win_rows, win_cols)

def tile_window(pos_cols, pos_rows, point_rates, point_amps, live_blocks):

    def add_block(block_index, running):
        offset = block_index * BP
        return running + block_field(lax.dynamic_slice_in_dim(pos_cols, offset, BP, 0), lax.dynamic_slice_in_dim(pos_rows, offset, BP, 0), lax.dynamic_slice_in_dim(point_rates, offset, BP, 0), lax.dynamic_slice_in_dim(point_amps, offset, BP, 1))
    empty_window = jnp.zeros((2, TH + 2 * RZ, TW + 2 * RZ), jnp.float32)
    return lax.fori_loop(0, live_blocks, add_block, empty_window)

def band_table(prop_rate, size_in, size_out, band_shift):
    offsets = jnp.arange(size_in, dtype=jnp.int32)[:, None] - jnp.arange(size_out, dtype=jnp.int32)[None, :] - band_shift
    inside = jnp.abs(offsets) <= HB
    distance = offsets.astype(jnp.float32)
    phases = prop_rate[0] * distance * distance
    kernel_scale = 1.0 / math.sqrt(2 * HB + 1)
    table_re = jnp.where(inside, jnp.cos(phases) * kernel_scale, 0.0)
    table_im = jnp.where(inside, jnp.sin(phases) * kernel_scale, 0.0)
    return jnp.concatenate([jnp.concatenate([table_re, table_im], 1), jnp.concatenate([-table_im, table_re], 1)], 0)

def propagate(extended, across_table, down_table):
    row_count = extended.shape[1]
    out_cols = across_table.shape[1] // 2
    side_by_side = jnp.concatenate([extended[0], extended[1]], axis=1)
    across = jnp.dot(side_by_side, across_table, precision=lax.Precision.HIGHEST, preferred_element_type=jnp.float32)
    stacked = across.reshape(row_count, 2, out_cols).transpose(1, 0, 2).reshape(2 * row_count, out_cols)
    result = lax.dot_general(down_table, stacked, (((0,), (0,)), ((), ())), precision=lax.Precision.HIGHEST, preferred_element_type=jnp.float32)
    return result.reshape(2, down_table.shape[1] // 2, out_cols)

def reference(counts, point_x, point_y, point_rate, point_amp, prop_rate):
    zero_index = jnp.int32(0)

    def place(tile_index, plane_sum):
        tile_row = tile_index // NTX
        tile_col = tile_index % NTX
        window = tile_window(point_x[tile_row, tile_col].astype(jnp.float32), point_y[tile_row, tile_col].astype(jnp.float32), point_rate[tile_row, tile_col], point_amp[tile_row, tile_col], counts[tile_row, tile_col])
        corner = (zero_index, (tile_row * TH).astype(jnp.int32), (tile_col * TW).astype(jnp.int32))
        current = lax.dynamic_slice(plane_sum, corner, (2, TH + 2 * RZ, TW + 2 * RZ))
        return lax.dynamic_update_slice(plane_sum, current + window, corner)
    plane_sum = jnp.zeros((2, NY + 2 * RZ, NX + 2 * RZ), jnp.float32)
    plane_sum = lax.fori_loop(jnp.int32(0), jnp.int32(NTY * NTX), place, plane_sum)
    field_plane = plane_sum[:, RZ:RZ + NY, RZ:RZ + NX]
    padded = jnp.pad(field_plane, ((0, 0), (HB, HB), (HB, HB)))
    across_table = band_table(prop_rate, TW + 2 * HB, TW, HB)
    down_table = band_table(prop_rate, TH + 2 * HB, TH, HB)

    def tile_out(tile_index):
        tile_row = tile_index // NTX
        tile_col = tile_index % NTX
        corner = (zero_index, (tile_row * TH).astype(jnp.int32), (tile_col * TW).astype(jnp.int32))
        extended = lax.dynamic_slice(padded, corner, (2, TH + 2 * HB, TW + 2 * HB))
        return propagate(extended, across_table, down_table)
    blocks = lax.map(tile_out, jnp.arange(NTY * NTX, dtype=jnp.int32))
    return blocks.reshape(NTY, NTX, 2, TH, TW).transpose(2, 0, 3, 1, 4).reshape(2, NY, NX)
```

```python
import functools
import math

import jax
import jax.numpy as jnp
from jax import lax
from jax.experimental import pallas as pl
from jax.experimental.pallas import tpu as pltpu
from jax.sharding import PartitionSpec as P

HB = 64
BP = 128
T = 128
SLAB = 32
FIELDS = 8
BF = jnp.bfloat16
F32 = jnp.float32


def fitted(func, degree):
    import numpy as np

    nodes = 0.125 - 0.125 * np.cos(np.pi * (np.arange(64) + 0.5) / 64)
    return [float(v) for v in np.polynomial.Polynomial.fit(nodes, func(nodes), degree).convert().coef]


def cos_values(s):
    import numpy as np

    return np.cos(np.pi * np.sqrt(s))


def sin_values(s):
    import numpy as np

    return np.sinc(np.sqrt(s)) * np.pi


COS = fitted(cos_values, 3)
SIN = fitted(sin_values, 3)


def poly(coefs, s):
    value = jnp.full_like(s, coefs[-1])
    for c in coefs[-2::-1]:
        value = value * s + c
    return value


def turn(t):
    f = t - jnp.floor(t + 0.5)
    s = f * f
    c = poly(COS, s)
    n = f * poly(SIN, s)
    n2 = n + n
    return 1.0 - n2 * n, n2 * c


def gen_axis(first, rate, place, amp):
    lane = lax.broadcasted_iota(jnp.int32, (SLAB, BP), 0).astype(F32) + float(first)
    m = jnp.abs(lane - place) - HB
    re, im = turn(rate * (m * m))
    if amp is not None:
        re, im = amp[0] * re - amp[1] * im, amp[0] * im + amp[1] * re
    return lane, re, im


def fill(dst, tiles, col, params, sign_rows):
    rate, pos, amp = params
    k = jnp.floor(pos * (1.0 / T))
    place = pos - k * T
    count = len(tiles)
    need_hi = [(k == j).astype(F32).astype(BF) for j in tiles]
    need_lo = [(k == j - 1).astype(F32).astype(BF) for j in tiles]
    for first in range(0, T, SLAB):
        lane, re, im = gen_axis(first, rate, place, amp)
        above = lane >= place
        below = lane <= place
        hi_re = jnp.where(above, re, 0.0).astype(BF)
        hi_im = jnp.where(above, im, 0.0).astype(BF)
        lo_re = jnp.where(below, re, 0.0).astype(BF)
        lo_im = jnp.where(below, im, 0.0).astype(BF)
        for n, j in enumerate(tiles):
            if j == 0:
                t_re, t_im = hi_re * need_hi[n], hi_im * need_hi[n]
            else:
                t_re = hi_re * need_hi[n] + lo_re * need_lo[n]
                t_im = hi_im * need_hi[n] + lo_im * need_lo[n]
            row = n * T + first
            if sign_rows:
                im_row = count * T + row
                dst[row : row + SLAB, col : col + BP] = t_re
                dst[row : row + SLAB, col + BP : col + 2 * BP] = -t_im
                dst[im_row : im_row + SLAB, col : col + BP] = t_im
                dst[im_row : im_row + SLAB, col + BP : col + 2 * BP] = t_re
            else:
                dst[row : row + SLAB, col : col + BP] = t_re
                dst[row : row + SLAB, col + BP : col + 2 * BP] = t_im


def add_source(pts, row_tiles, col_tiles, dst_row, dst_col, chunk, left, right, acc):
    count = jnp.max(pts[5:6, :BP]).astype(jnp.int32)
    nr, nc = len(row_tiles), len(col_tiles)

    @pl.loop(0, (count + chunk - 1) // chunk)
    def _(step):
        for b in range(chunk):
            offset = pl.multiple_of((step * chunk + b) * BP, BP)
            x = pts[0:1, pl.ds(offset, BP)]
            y = pts[1:2, pl.ds(offset, BP)]
            rate = pts[2:3, pl.ds(offset, BP)] * (0.5 / math.pi)
            amp = (pts[3:4, pl.ds(offset, BP)], pts[4:5, pl.ds(offset, BP)])
            fill(left, row_tiles, 2 * BP * b, (rate, y, None), True)
            fill(right, col_tiles, 2 * BP * b, (rate, x, amp), False)
        product = lax.dot_general(
            left[: 2 * nr * T, : 2 * BP * chunk],
            right[: nc * T, : 2 * BP * chunk],
            (((1,), (1,)), ((), ())),
            preferred_element_type=F32,
        )
        rows = slice(dst_row * T, (dst_row + nr) * T)
        cols = slice(dst_col * T, (dst_col + nc) * T)
        acc[0, rows, cols] += product[: nr * T]
        acc[1, rows, cols] += product[nr * T :]


def split(value):
    high = value.astype(BF)
    return high, (value - high.astype(F32)).astype(BF)


def band(prop, in_dim):
    shape = (2 * T, T) if in_dim == 0 else (T, 2 * T)
    offset = (
        lax.broadcasted_iota(jnp.int32, shape, in_dim)
        - lax.broadcasted_iota(jnp.int32, shape, 1 - in_dim)
        - HB
    ).astype(F32)
    re, im = turn(prop * (0.5 / math.pi) * (offset * offset))
    inside = jnp.abs(offset) <= HB
    scale = 1.0 / math.sqrt(2 * HB + 1)
    return jnp.where(inside, re * scale, 0.0), jnp.where(inside, im * scale, 0.0)


def field_kernel(prop, edges, own, near, out, left, right, acc, across):
    rows_n, cols_n = acc.shape[1] // T, acc.shape[2] // T
    acc[...] = jnp.zeros_like(acc)
    all_rows, all_cols = list(range(rows_n)), list(range(cols_n))
    add_source(own, all_rows, all_cols, 0, 0, 4, left, right, acc)
    pick_r = {-1: ([rows_n - 1], 0), 0: (all_rows, 0), 1: ([0], rows_n - 1)}
    pick_c = {-1: ([cols_n - 1], 0), 0: (all_cols, 0), 1: ([0], cols_n - 1)}
    for index, (dy, dx) in enumerate(SHIFTS):
        (row_tiles, dst_row), (col_tiles, dst_col) = pick_r[dy], pick_c[dx]
        add_source(near.at[index], row_tiles, col_tiles, dst_row, dst_col, 1, left, right, acc)

    ends = (
        (slice(0, HB), slice(None)),
        (slice(rows_n * T - HB, rows_n * T), slice(None)),
    )
    for e, (r, c) in enumerate(ends):

        @pl.when(edges[e] == 1)
        def _():
            acc[:, r, c] = jnp.zeros_like(acc[:, r, c])

    lanes = lax.broadcasted_iota(jnp.int32, (1, T), 1)
    for e, col, keep in ((2, 0, lanes >= HB), (3, (cols_n - 1) * T, lanes < T - HB)):

        @pl.when(edges[e] == 1)
        def _():
            acc[:, :, col : col + T] = jnp.where(keep[None], acc[:, :, col : col + T], 0.0)

    re, im = band(prop[0], 0)
    table = jnp.concatenate(
        [jnp.concatenate([re, im], 1), jnp.concatenate([-im, re], 1)], 0
    )
    tables = split(table)
    for j in range(cols_n - 1):
        cols = slice(j * T, (j + 2) * T)
        data = jnp.concatenate([acc[0, :, cols], acc[1, :, cols]], 1).astype(BF)
        result = sum(jnp.dot(data, t, preferred_element_type=F32) for t in tables)
        across[0, :, j * T : (j + 1) * T] = result[:, :T].astype(BF)
        across[1, :, j * T : (j + 1) * T] = result[:, T:].astype(BF)

    re, im = band(prop[0], 1)
    table = jnp.concatenate(
        [jnp.concatenate([re, -im], 1), jnp.concatenate([im, re], 1)], 0
    )
    tables = split(table)
    for q in range(rows_n - 1):
        rows = slice(q * T, (q + 2) * T)
        data = jnp.concatenate([across[0, rows, :], across[1, rows, :]], 0)
        result = sum(jnp.dot(t, data, preferred_element_type=F32) for t in tables)
        out[0, q * T : (q + 1) * T, :] = result[:T]
        out[1, q * T : (q + 1) * T, :] = result[T:]


SHIFTS = ((0, -1), (0, 1), (-1, 0), (1, 0), (-1, -1), (-1, 1), (1, -1), (1, 1))


def on_device(th, tw, counts, point_x, point_y, point_rate, point_amp, prop_rate):
    axes = ("col", "row", "sub")
    n_row = lax.axis_size("row") * lax.axis_size("sub")
    n_col = lax.axis_size("col")
    points = point_x.shape[-1]
    live = jnp.arange(points, dtype=jnp.int32) < counts[0, 0] * BP
    own = jnp.stack(
        [
            point_x[0, 0].astype(F32),
            point_y[0, 0].astype(F32),
            point_rate[0, 0],
            jnp.where(live, point_amp[0, 0, 0], 0.0),
            jnp.where(live, point_amp[0, 0, 1], 0.0),
            jnp.full((points,), counts[0, 0].astype(F32)),
            jnp.zeros((points,), F32),
            jnp.zeros((points,), F32),
        ]
    )
    near = []
    for dy, dx in SHIFTS:
        pairs = [
            ((x + dx) * n_row + y + dy, x * n_row + y)
            for y in range(n_row)
            for x in range(n_col)
            if 0 <= y + dy < n_row and 0 <= x + dx < n_col
        ]
        near.append(lax.ppermute(own, axes, pairs))
    near = jnp.stack(near)
    at_row = lax.axis_index("row") * lax.axis_size("sub") + lax.axis_index("sub")
    at_col = lax.axis_index("col")
    edges = jnp.stack(
        [at_row == 0, at_row == n_row - 1, at_col == 0, at_col == n_col - 1]
    ).astype(jnp.int32)
    wide, high = tw + 2 * HB, th + 2 * HB
    vmem = pl.BlockSpec(memory_space=pltpu.VMEM)
    smem = pl.BlockSpec(memory_space=pltpu.SMEM)
    return pl.pallas_call(
        field_kernel,
        out_shape=jax.ShapeDtypeStruct((2, th, tw), F32),
        in_specs=[smem, smem, vmem, vmem],
        out_specs=vmem,
        scratch_shapes=[
            pltpu.VMEM((2 * high, 8 * BP), BF),
            pltpu.VMEM((wide, 8 * BP), BF),
            pltpu.VMEM((2, high, wide), F32),
            pltpu.VMEM((2, high, tw), BF),
        ],
        compiler_params=pltpu.CompilerParams(vmem_limit_bytes=48 * 1024 * 1024),
    )(prop_rate, edges, own, near)


def solution(mesh):
    th, tw = 256, 512
    return jax.shard_map(
        functools.partial(on_device, th, tw),
        mesh=mesh,
        in_specs=(
            P(("grp", "row", "sub"), "col"),
            P(("grp", "row", "sub"), "col", None),
            P(("grp", "row", "sub"), "col", None),
            P(("grp", "row", "sub"), "col", None),
            P(("grp", "row", "sub"), "col", None, None),
            P(),
        ),
        out_specs=P(None, ("grp", "row", "sub"), "col"),
        check_vma=False,
    )
```

```python
import functools
import math

import jax
import jax.numpy as jnp
from jax import lax
from jax.experimental import pallas as pl
from jax.experimental.pallas import tpu as pltpu
from jax.sharding import PartitionSpec as P

HB = 64
BP = 128
T = 128
SLAB = 32
FIELDS = 8
BF = jnp.bfloat16
F32 = jnp.float32


def fitted(func, degree):
    import numpy as np

    nodes = 0.125 - 0.125 * np.cos(np.pi * (np.arange(64) + 0.5) / 64)
    return [float(v) for v in np.polynomial.Polynomial.fit(nodes, func(nodes), degree).convert().coef]


def cos_values(s):
    import numpy as np

    return np.cos(np.pi * np.sqrt(s))


def sin_values(s):
    import numpy as np

    return np.sinc(np.sqrt(s)) * np.pi


COS = fitted(cos_values, 3)
SIN = fitted(sin_values, 3)


def poly(coefs, s):
    value = jnp.full_like(s, coefs[-1])
    for c in coefs[-2::-1]:
        value = value * s + c
    return value


def turn(t):
    f = t - jnp.floor(t + 0.5)
    s = f * f
    c = poly(COS, s)
    n = f * poly(SIN, s)
    n2 = n + n
    return 1.0 - n2 * n, n2 * c


def gen_axis(first, rate, place, amp):
    lane = lax.broadcasted_iota(jnp.int32, (SLAB, BP), 0).astype(F32) + float(first)
    m = jnp.abs(lane - place) - HB
    re, im = turn(rate * (m * m))
    if amp is not None:
        re, im = amp[0] * re - amp[1] * im, amp[0] * im + amp[1] * re
    return lane, re, im


def fill(dst, tiles, col, params, sign_rows):
    rate, pos, amp = params
    k = jnp.floor(pos * (1.0 / T))
    place = pos - k * T
    count = len(tiles)
    need_hi = [(k == j).astype(F32).astype(BF) for j in tiles]
    need_lo = [(k == j - 1).astype(F32).astype(BF) for j in tiles]
    for first in range(0, T, SLAB):
        lane, re, im = gen_axis(first, rate, place, amp)
        above = lane >= place
        below = lane <= place
        hi_re = jnp.where(above, re, 0.0).astype(BF)
        hi_im = jnp.where(above, im, 0.0).astype(BF)
        lo_re = jnp.where(below, re, 0.0).astype(BF)
        lo_im = jnp.where(below, im, 0.0).astype(BF)
        for n, j in enumerate(tiles):
            if j == 0:
                t_re, t_im = hi_re * need_hi[n], hi_im * need_hi[n]
            else:
                t_re = hi_re * need_hi[n] + lo_re * need_lo[n]
                t_im = hi_im * need_hi[n] + lo_im * need_lo[n]
            row = n * T + first
            if sign_rows:
                im_row = count * T + row
                dst[row : row + SLAB, col : col + BP] = t_re
                dst[row : row + SLAB, col + BP : col + 2 * BP] = -t_im
                dst[im_row : im_row + SLAB, col : col + BP] = t_im
                dst[im_row : im_row + SLAB, col + BP : col + 2 * BP] = t_re
            else:
                dst[row : row + SLAB, col : col + BP] = t_re
                dst[row : row + SLAB, col + BP : col + 2 * BP] = t_im


def add_source(pts, row_tiles, col_tiles, dst_row, dst_col, chunk, left, right, acc):
    count = jnp.max(pts[5:6, :BP]).astype(jnp.int32)
    nr, nc = len(row_tiles), len(col_tiles)

    @pl.loop(0, (count + chunk - 1) // chunk)
    def _(step):
        for b in range(chunk):
            offset = pl.multiple_of((step * chunk + b) * BP, BP)
            x = pts[0:1, pl.ds(offset, BP)]
            y = pts[1:2, pl.ds(offset, BP)]
            rate = pts[2:3, pl.ds(offset, BP)] * (0.5 / math.pi)
            amp = (pts[3:4, pl.ds(offset, BP)], pts[4:5, pl.ds(offset, BP)])
            fill(left, row_tiles, 2 * BP * b, (rate, y, None), True)
            fill(right, col_tiles, 2 * BP * b, (rate, x, amp), False)
        product = lax.dot_general(
            left[: 2 * nr * T, : 2 * BP * chunk],
            right[: nc * T, : 2 * BP * chunk],
            (((1,), (1,)), ((), ())),
            preferred_element_type=F32,
        )
        rows = slice(dst_row * T, (dst_row + nr) * T)
        cols = slice(dst_col * T, (dst_col + nc) * T)
        acc[0, rows, cols] += product[: nr * T]
        acc[1, rows, cols] += product[nr * T :]


def split(value):
    high = value.astype(BF)
    return high, (value - high.astype(F32)).astype(BF)


def band(prop, in_dim):
    shape = (2 * T, T) if in_dim == 0 else (T, 2 * T)
    offset = (
        lax.broadcasted_iota(jnp.int32, shape, in_dim)
        - lax.broadcasted_iota(jnp.int32, shape, 1 - in_dim)
        - HB
    ).astype(F32)
    re, im = turn(prop * (0.5 / math.pi) * (offset * offset))
    inside = jnp.abs(offset) <= HB
    scale = 1.0 / math.sqrt(2 * HB + 1)
    return jnp.where(inside, re * scale, 0.0), jnp.where(inside, im * scale, 0.0)


def field_kernel(prop, own, near, out, left, right, acc, across):
    rows_n, cols_n = acc.shape[1] // T, acc.shape[2] // T
    acc[...] = jnp.zeros_like(acc)
    all_rows, all_cols = list(range(rows_n)), list(range(cols_n))
    add_source(own, all_rows, all_cols, 0, 0, 4, left, right, acc)
    pick_r = {-1: ([rows_n - 1], 0), 0: (all_rows, 0), 1: ([0], rows_n - 1)}
    pick_c = {-1: ([cols_n - 1], 0), 0: (all_cols, 0), 1: ([0], cols_n - 1)}
    for index, (dy, dx) in enumerate(SHIFTS):
        (row_tiles, dst_row), (col_tiles, dst_col) = pick_r[dy], pick_c[dx]
        add_source(near.at[index], row_tiles, col_tiles, dst_row, dst_col, 1, left, right, acc)

    _, at_row, n_row, at_col, n_col = position()
    edges = (at_row == 0, at_row == n_row - 1, at_col == 0, at_col == n_col - 1)
    ends = (
        (slice(0, HB), slice(None)),
        (slice(rows_n * T - HB, rows_n * T), slice(None)),
    )
    for e, (r, c) in enumerate(ends):

        @pl.when(edges[e])
        def _():
            acc[:, r, c] = jnp.zeros_like(acc[:, r, c])

    lanes = lax.broadcasted_iota(jnp.int32, (1, T), 1)
    for e, col, keep in ((2, 0, lanes >= HB), (3, (cols_n - 1) * T, lanes < T - HB)):

        @pl.when(edges[e])
        def _():
            acc[:, :, col : col + T] = jnp.where(keep[None], acc[:, :, col : col + T], 0.0)

    re, im = band(prop[0], 0)
    table = jnp.concatenate(
        [jnp.concatenate([re, im], 1), jnp.concatenate([-im, re], 1)], 0
    )
    tables = split(table)
    for j in range(cols_n - 1):
        cols = slice(j * T, (j + 2) * T)
        data = jnp.concatenate([acc[0, :, cols], acc[1, :, cols]], 1).astype(BF)
        result = sum(jnp.dot(data, t, preferred_element_type=F32) for t in tables)
        across[0, :, j * T : (j + 1) * T] = result[:, :T].astype(BF)
        across[1, :, j * T : (j + 1) * T] = result[:, T:].astype(BF)

    re, im = band(prop[0], 1)
    table = jnp.concatenate(
        [jnp.concatenate([re, -im], 1), jnp.concatenate([im, re], 1)], 0
    )
    tables = split(table)
    for q in range(rows_n - 1):
        rows = slice(q * T, (q + 2) * T)
        data = jnp.concatenate([across[0, rows, :], across[1, rows, :]], 0)
        result = sum(jnp.dot(t, data, preferred_element_type=F32) for t in tables)
        out[0, q * T : (q + 1) * T, :] = result[:T]
        out[1, q * T : (q + 1) * T, :] = result[T:]


SHIFTS = ((0, -1), (0, 1), (-1, 0), (1, 0), (-1, -1), (-1, 1), (1, -1), (1, 1))


def position():
    n_sub = lax.axis_size("sub")
    at_row = lax.axis_index("row") * n_sub + lax.axis_index("sub")
    return n_sub, at_row, lax.axis_size("row") * n_sub, lax.axis_index("col"), lax.axis_size("col")


def exchange_kernel(counts, px, py, pr, pa, own_out, near_out, own, near, send, recv):
    n_sub, at_row, n_row, at_col, n_col = position()

    def neighbour(dy, dx):
        y, x = at_row + dy, at_col + dx
        there = (y >= 0) & (y < n_row) & (x >= 0) & (x < n_col)
        return there, (lax.axis_index("grp"), x, lax.div(y, n_sub), lax.rem(y, n_sub))

    barrier = pltpu.get_barrier_semaphore()
    for shift in SHIFTS:
        there, device = neighbour(*shift)

        @pl.when(there)
        def _():
            pl.semaphore_signal(
                barrier, inc=1, device_id=device, device_id_type=pl.DeviceIdType.MESH
            )

    count = counts[0, 0]
    live = lax.broadcasted_iota(jnp.int32, px.shape, 1) < count * BP
    own[0:1] = px[...].astype(F32)
    own[1:2] = py[...].astype(F32)
    own[2:3] = pr[...]
    own[3:4] = jnp.where(live, pa[0:1], 0.0)
    own[4:5] = jnp.where(live, pa[1:2], 0.0)
    own[5:8] = jnp.broadcast_to(count.astype(F32), (3, px.shape[1]))
    own_out[...] = own[...]

    tall = 3 - (at_row == 0).astype(jnp.int32) - (at_row == n_row - 1).astype(jnp.int32)
    broad = 3 - (at_col == 0).astype(jnp.int32) - (at_col == n_col - 1).astype(jnp.int32)
    pl.semaphore_wait(barrier, tall * broad - 1)

    def copy(index, shift):
        there, device = neighbour(*shift)
        return there, pltpu.make_async_remote_copy(
            src_ref=own,
            dst_ref=near.at[index],
            send_sem=send.at[index],
            recv_sem=recv.at[index],
            device_id=device,
            device_id_type=pl.DeviceIdType.MESH,
        )

    back = [SHIFTS.index((-dy, -dx)) for dy, dx in SHIFTS]
    for index, shift in enumerate(SHIFTS):
        there, there_copy = copy(back[index], shift)

        @pl.when(there)
        def _():
            there_copy.start()

    for index, shift in enumerate(SHIFTS):
        there, _ = neighbour(*shift)
        _, incoming = copy(index, shift)

        @pl.when(there)
        def _():
            incoming.wait_recv()
            near_out[index] = near[index]

        @pl.when(jnp.logical_not(there))
        def _():
            near_out[index] = jnp.zeros_like(near_out[index])

    for index, shift in enumerate(SHIFTS):
        there, there_copy = copy(back[index], shift)

        @pl.when(there)
        def _():
            there_copy.wait_send()


def on_device(th, tw, counts, point_x, point_y, point_rate, point_amp, prop_rate):
    points = point_x.shape[-1]
    vmem = pl.BlockSpec(memory_space=pltpu.VMEM)
    smem = pl.BlockSpec(memory_space=pltpu.SMEM)
    own, near = pl.pallas_call(
        exchange_kernel,
        out_shape=[
            jax.ShapeDtypeStruct((FIELDS, points), F32),
            jax.ShapeDtypeStruct((len(SHIFTS), FIELDS, points), F32),
        ],
        in_specs=[smem, vmem, vmem, vmem, vmem],
        out_specs=[vmem, vmem],
        scratch_shapes=[
            pltpu.VMEM((FIELDS, points), F32),
            pltpu.VMEM((len(SHIFTS), FIELDS, points), F32),
            pltpu.SemaphoreType.DMA((len(SHIFTS),)),
            pltpu.SemaphoreType.DMA((len(SHIFTS),)),
        ],
        compiler_params=pltpu.CompilerParams(collective_id=0, has_side_effects=True),
    )(counts, point_x[0], point_y[0], point_rate[0], point_amp[0, 0])
    wide, high = tw + 2 * HB, th + 2 * HB
    return pl.pallas_call(
        field_kernel,
        out_shape=jax.ShapeDtypeStruct((2, th, tw), F32),
        in_specs=[smem, vmem, vmem],
        out_specs=vmem,
        scratch_shapes=[
            pltpu.VMEM((2 * high, 8 * BP), BF),
            pltpu.VMEM((wide, 8 * BP), BF),
            pltpu.VMEM((2, high, wide), F32),
            pltpu.VMEM((2, high, tw), BF),
        ],
        compiler_params=pltpu.CompilerParams(vmem_limit_bytes=48 * 1024 * 1024),
    )(prop_rate, own, near)


def solution(mesh):
    th, tw = 256, 512
    return jax.shard_map(
        functools.partial(on_device, th, tw),
        mesh=mesh,
        in_specs=(
            P(("grp", "row", "sub"), "col"),
            P(("grp", "row", "sub"), "col", None),
            P(("grp", "row", "sub"), "col", None),
            P(("grp", "row", "sub"), "col", None),
            P(("grp", "row", "sub"), "col", None, None),
            P(),
        ),
        out_specs=P(None, ("grp", "row", "sub"), "col"),
        check_vma=False,
    )
```

```python
import functools
import math

import jax
import jax.numpy as jnp
from jax import lax
from jax.experimental import pallas as pl
from jax.experimental.pallas import tpu as pltpu
from jax.sharding import PartitionSpec as P

HB = 64
BP = 128
T = 128
SLAB = 32
FIELDS = 8
BF = jnp.bfloat16
F32 = jnp.float32


def fitted(func, degree):
    import numpy as np

    nodes = 0.125 - 0.125 * np.cos(np.pi * (np.arange(64) + 0.5) / 64)
    return [float(v) for v in np.polynomial.Polynomial.fit(nodes, func(nodes), degree).convert().coef]


def cos_values(s):
    import numpy as np

    return np.cos(np.pi * np.sqrt(s))


def sin_values(s):
    import numpy as np

    return np.sinc(np.sqrt(s)) * np.pi


COS = fitted(cos_values, 3)
SIN = fitted(sin_values, 3)


def poly(coefs, s):
    value = jnp.full_like(s, coefs[-1])
    for c in coefs[-2::-1]:
        value = value * s + c
    return value


def turn(t):
    f = t - jnp.floor(t + 0.5)
    s = f * f
    c = poly(COS, s)
    n = f * poly(SIN, s)
    n2 = n + n
    return 1.0 - n2 * n, n2 * c


def gen_axis(first, rate, place, amp):
    lane = lax.broadcasted_iota(jnp.int32, (SLAB, BP), 0).astype(F32) + float(first)
    m = jnp.abs(lane - place) - HB
    re, im = turn(rate * (m * m))
    if amp is not None:
        re, im = amp[0] * re - amp[1] * im, amp[0] * im + amp[1] * re
    return lane, re, im


def fill(dst, tiles, col, params, sign_rows):
    rate, pos, amp = params
    k = jnp.floor(pos * (1.0 / T))
    place = pos - k * T
    count = len(tiles)
    need_hi = [(k == j).astype(F32).astype(BF) for j in tiles]
    need_lo = [(k == j - 1).astype(F32).astype(BF) for j in tiles]
    for first in range(0, T, SLAB):
        lane, re, im = gen_axis(first, rate, place, amp)
        above = lane >= place
        below = lane <= place
        hi_re = jnp.where(above, re, 0.0).astype(BF)
        hi_im = jnp.where(above, im, 0.0).astype(BF)
        lo_re = jnp.where(below, re, 0.0).astype(BF)
        lo_im = jnp.where(below, im, 0.0).astype(BF)
        for n, j in enumerate(tiles):
            if j == 0:
                t_re, t_im = hi_re * need_hi[n], hi_im * need_hi[n]
            else:
                t_re = hi_re * need_hi[n] + lo_re * need_lo[n]
                t_im = hi_im * need_hi[n] + lo_im * need_lo[n]
            row = n * T + first
            if sign_rows:
                im_row = count * T + row
                dst[row : row + SLAB, col : col + BP] = t_re
                dst[row : row + SLAB, col + BP : col + 2 * BP] = -t_im
                dst[im_row : im_row + SLAB, col : col + BP] = t_im
                dst[im_row : im_row + SLAB, col + BP : col + 2 * BP] = t_re
            else:
                dst[row : row + SLAB, col : col + BP] = t_re
                dst[row : row + SLAB, col + BP : col + 2 * BP] = t_im


def compact(near, packed, spans):
    total = near.shape[2]
    lane = lax.broadcasted_iota(jnp.int32, (len(SHIFTS), total), 1)
    which = lax.broadcasted_iota(jnp.int32, (len(SHIFTS), total), 0)

    def bound(pick):
        value = jnp.zeros((len(SHIFTS), total), F32)
        for i, span in enumerate(spans):
            value = jnp.where(which == i, float(span[pick]), value)
        return value

    data = [near[:, f, :] for f in range(5)]
    keep = lane.astype(F32) < near[:, 5, :] * float(BP)
    keep = keep & (data[0] >= bound(0)) & (data[0] < bound(1))
    keep = keep & (data[1] >= bound(2)) & (data[1] < bound(3))
    flag = keep.astype(F32)
    numbers = [jnp.sum(flag[i : i + 1]).astype(jnp.int32) for i in range(len(SHIFTS))]
    gaps = jnp.where(keep, 0, 1)
    step = 1
    while step < total:
        gaps = gaps + jnp.where(lane >= step, pltpu.roll(gaps, step, 1), 0)
        step *= 2
    move = jnp.where(keep, gaps, 0)
    data = [jnp.where(keep, d, 0.0) for d in data]
    step = 1
    while step < total:
        come = pltpu.roll(move, total - step, 1)
        arrives = (come & step) != 0
        leaves = (move & step) != 0
        move = jnp.where(arrives, come, jnp.where(leaves, 0, move))
        data = [
            jnp.where(arrives, pltpu.roll(d, total - step, 1), jnp.where(leaves, 0.0, d))
            for d in data
        ]
        step *= 2
    for f in range(5):
        packed[f] = data[f]
    return numbers


def add_source(pts, count, row_tiles, col_tiles, dst_row, dst_col, chunk, left, right, acc):
    nr, nc = len(row_tiles), len(col_tiles)

    @pl.loop(0, (count + chunk - 1) // chunk)
    def _(step):
        for b in range(chunk):
            offset = pl.multiple_of((step * chunk + b) * BP, BP)
            x = pts(0, offset)
            y = pts(1, offset)
            rate = pts(2, offset) * (0.5 / math.pi)
            amp = (pts(3, offset), pts(4, offset))
            fill(left, row_tiles, 2 * BP * b, (rate, y, None), True)
            fill(right, col_tiles, 2 * BP * b, (rate, x, amp), False)
        product = lax.dot_general(
            left[: 2 * nr * T, : 2 * BP * chunk],
            right[: nc * T, : 2 * BP * chunk],
            (((1,), (1,)), ((), ())),
            preferred_element_type=F32,
        )
        rows = slice(dst_row * T, (dst_row + nr) * T)
        cols = slice(dst_col * T, (dst_col + nc) * T)
        acc[0, rows, cols] += product[: nr * T]
        acc[1, rows, cols] += product[nr * T :]


def split(value):
    high = value.astype(BF)
    return high, (value - high.astype(F32)).astype(BF)


def band(prop, in_dim):
    shape = (2 * T, T) if in_dim == 0 else (T, 2 * T)
    offset = (
        lax.broadcasted_iota(jnp.int32, shape, in_dim)
        - lax.broadcasted_iota(jnp.int32, shape, 1 - in_dim)
        - HB
    ).astype(F32)
    re, im = turn(prop * (0.5 / math.pi) * (offset * offset))
    inside = jnp.abs(offset) <= HB
    scale = 1.0 / math.sqrt(2 * HB + 1)
    return jnp.where(inside, re * scale, 0.0), jnp.where(inside, im * scale, 0.0)


def field_kernel(prop, own, near, out, left, right, acc, across, packed):
    rows_n, cols_n = acc.shape[1] // T, acc.shape[2] // T
    acc[...] = jnp.zeros_like(acc)
    all_rows, all_cols = list(range(rows_n)), list(range(cols_n))
    wide, high = float((cols_n - 1) * T), float((rows_n - 1) * T)
    reach_c = {-1: (wide - T, wide), 0: (0.0, wide), 1: (0.0, float(T))}
    reach_r = {-1: (high - T, high), 0: (0.0, high), 1: (0.0, float(T))}
    numbers = compact(near, packed, [reach_c[dx] + reach_r[dy] for dy, dx in SHIFTS])

    def own_points(f, offset):
        return own[f : f + 1, pl.ds(offset, BP)]

    count = jnp.max(own[5:6, :BP]).astype(jnp.int32)
    add_source(own_points, count, all_rows, all_cols, 0, 0, 4, left, right, acc)
    pick_r = {-1: ([rows_n - 1], 0), 0: (all_rows, 0), 1: ([0], rows_n - 1)}
    pick_c = {-1: ([cols_n - 1], 0), 0: (all_cols, 0), 1: ([0], cols_n - 1)}
    for index, (dy, dx) in enumerate(SHIFTS):
        (row_tiles, dst_row), (col_tiles, dst_col) = pick_r[dy], pick_c[dx]

        def points(f, offset):
            return packed[f, index : index + 1, pl.ds(offset, BP)]

        blocks = (numbers[index] + BP - 1) // BP
        add_source(points, blocks, row_tiles, col_tiles, dst_row, dst_col, 1, left, right, acc)

    _, at_row, n_row, at_col, n_col = position()
    edges = (at_row == 0, at_row == n_row - 1, at_col == 0, at_col == n_col - 1)
    ends = (
        (slice(0, HB), slice(None)),
        (slice(rows_n * T - HB, rows_n * T), slice(None)),
    )
    for e, (r, c) in enumerate(ends):

        @pl.when(edges[e])
        def _():
            acc[:, r, c] = jnp.zeros_like(acc[:, r, c])

    lanes = lax.broadcasted_iota(jnp.int32, (1, T), 1)
    for e, col, keep in ((2, 0, lanes >= HB), (3, (cols_n - 1) * T, lanes < T - HB)):

        @pl.when(edges[e])
        def _():
            acc[:, :, col : col + T] = jnp.where(keep[None], acc[:, :, col : col + T], 0.0)

    re, im = band(prop[0], 0)
    table = jnp.concatenate(
        [jnp.concatenate([re, im], 1), jnp.concatenate([-im, re], 1)], 0
    )
    tables = split(table)
    for j in range(cols_n - 1):
        cols = slice(j * T, (j + 2) * T)
        data = jnp.concatenate([acc[0, :, cols], acc[1, :, cols]], 1).astype(BF)
        result = sum(jnp.dot(data, t, preferred_element_type=F32) for t in tables)
        across[0, :, j * T : (j + 1) * T] = result[:, :T].astype(BF)
        across[1, :, j * T : (j + 1) * T] = result[:, T:].astype(BF)

    re, im = band(prop[0], 1)
    table = jnp.concatenate(
        [jnp.concatenate([re, -im], 1), jnp.concatenate([im, re], 1)], 0
    )
    tables = split(table)
    for q in range(rows_n - 1):
        rows = slice(q * T, (q + 2) * T)
        data = jnp.concatenate([across[0, rows, :], across[1, rows, :]], 0)
        result = sum(jnp.dot(t, data, preferred_element_type=F32) for t in tables)
        out[0, q * T : (q + 1) * T, :] = result[:T]
        out[1, q * T : (q + 1) * T, :] = result[T:]


SHIFTS = ((0, -1), (0, 1), (-1, 0), (1, 0), (-1, -1), (-1, 1), (1, -1), (1, 1))


def position():
    n_sub = lax.axis_size("sub")
    at_row = lax.axis_index("row") * n_sub + lax.axis_index("sub")
    return n_sub, at_row, lax.axis_size("row") * n_sub, lax.axis_index("col"), lax.axis_size("col")


def exchange_kernel(counts, px, py, pr, pa, own_out, near_out, own, near, send, recv):
    n_sub, at_row, n_row, at_col, n_col = position()

    def neighbour(dy, dx):
        y, x = at_row + dy, at_col + dx
        there = (y >= 0) & (y < n_row) & (x >= 0) & (x < n_col)
        return there, (lax.axis_index("grp"), x, lax.div(y, n_sub), lax.rem(y, n_sub))

    barrier = pltpu.get_barrier_semaphore()
    for shift in SHIFTS:
        there, device = neighbour(*shift)

        @pl.when(there)
        def _():
            pl.semaphore_signal(
                barrier, inc=1, device_id=device, device_id_type=pl.DeviceIdType.MESH
            )

    count = counts[0, 0]
    live = lax.broadcasted_iota(jnp.int32, px.shape, 1) < count * BP
    own[0:1] = px[...].astype(F32)
    own[1:2] = py[...].astype(F32)
    own[2:3] = pr[...]
    own[3:4] = jnp.where(live, pa[0:1], 0.0)
    own[4:5] = jnp.where(live, pa[1:2], 0.0)
    own[5:8] = jnp.broadcast_to(count.astype(F32), (3, px.shape[1]))
    own_out[...] = own[...]

    tall = 3 - (at_row == 0).astype(jnp.int32) - (at_row == n_row - 1).astype(jnp.int32)
    broad = 3 - (at_col == 0).astype(jnp.int32) - (at_col == n_col - 1).astype(jnp.int32)
    pl.semaphore_wait(barrier, tall * broad - 1)

    def copy(index, shift):
        there, device = neighbour(*shift)
        return there, pltpu.make_async_remote_copy(
            src_ref=own,
            dst_ref=near.at[index],
            send_sem=send.at[index],
            recv_sem=recv.at[index],
            device_id=device,
            device_id_type=pl.DeviceIdType.MESH,
        )

    back = [SHIFTS.index((-dy, -dx)) for dy, dx in SHIFTS]
    for index, shift in enumerate(SHIFTS):
        there, there_copy = copy(back[index], shift)

        @pl.when(there)
        def _():
            there_copy.start()

    for index, shift in enumerate(SHIFTS):
        there, _ = neighbour(*shift)
        _, incoming = copy(index, shift)

        @pl.when(there)
        def _():
            incoming.wait_recv()
            near_out[index] = near[index]

        @pl.when(jnp.logical_not(there))
        def _():
            near_out[index] = jnp.zeros_like(near_out[index])

    for index, shift in enumerate(SHIFTS):
        there, there_copy = copy(back[index], shift)

        @pl.when(there)
        def _():
            there_copy.wait_send()


def on_device(th, tw, counts, point_x, point_y, point_rate, point_amp, prop_rate):
    points = point_x.shape[-1]
    vmem = pl.BlockSpec(memory_space=pltpu.VMEM)
    smem = pl.BlockSpec(memory_space=pltpu.SMEM)
    own, near = pl.pallas_call(
        exchange_kernel,
        out_shape=[
            jax.ShapeDtypeStruct((FIELDS, points), F32),
            jax.ShapeDtypeStruct((len(SHIFTS), FIELDS, points), F32),
        ],
        in_specs=[smem, vmem, vmem, vmem, vmem],
        out_specs=[vmem, vmem],
        scratch_shapes=[
            pltpu.VMEM((FIELDS, points), F32),
            pltpu.VMEM((len(SHIFTS), FIELDS, points), F32),
            pltpu.SemaphoreType.DMA((len(SHIFTS),)),
            pltpu.SemaphoreType.DMA((len(SHIFTS),)),
        ],
        compiler_params=pltpu.CompilerParams(collective_id=0, has_side_effects=True),
    )(counts, point_x[0], point_y[0], point_rate[0], point_amp[0, 0])
    wide, high = tw + 2 * HB, th + 2 * HB
    return pl.pallas_call(
        field_kernel,
        out_shape=jax.ShapeDtypeStruct((2, th, tw), F32),
        in_specs=[smem, vmem, vmem],
        out_specs=vmem,
        scratch_shapes=[
            pltpu.VMEM((2 * high, 8 * BP), BF),
            pltpu.VMEM((wide, 8 * BP), BF),
            pltpu.VMEM((2, high, wide), F32),
            pltpu.VMEM((2, high, tw), BF),
            pltpu.VMEM((5, len(SHIFTS), points), F32),
        ],
        compiler_params=pltpu.CompilerParams(vmem_limit_bytes=48 * 1024 * 1024),
    )(prop_rate, own, near)


def solution(mesh):
    th, tw = 256, 512
    return jax.shard_map(
        functools.partial(on_device, th, tw),
        mesh=mesh,
        in_specs=(
            P(("grp", "row", "sub"), "col"),
            P(("grp", "row", "sub"), "col", None),
            P(("grp", "row", "sub"), "col", None),
            P(("grp", "row", "sub"), "col", None),
            P(("grp", "row", "sub"), "col", None, None),
            P(),
        ),
        out_specs=P(None, ("grp", "row", "sub"), "col"),
        check_vma=False,
    )
```

```python
import functools
import math

import jax
import jax.numpy as jnp
from jax import lax
from jax.experimental import pallas as pl
from jax.experimental.pallas import tpu as pltpu
from jax.sharding import PartitionSpec as P

HB = 64
BP = 128
T = 128
SLAB = 32
FIELDS = 8
BF = jnp.bfloat16
F32 = jnp.float32


def fitted(func, degree):
    import numpy as np

    nodes = 0.125 - 0.125 * np.cos(np.pi * (np.arange(64) + 0.5) / 64)
    return [float(v) for v in np.polynomial.Polynomial.fit(nodes, func(nodes), degree).convert().coef]


def cos_values(s):
    import numpy as np

    return np.cos(np.pi * np.sqrt(s))


def sin_values(s):
    import numpy as np

    return np.sinc(np.sqrt(s)) * np.pi


COS = fitted(cos_values, 3)
SIN = fitted(sin_values, 3)


def poly(coefs, s):
    value = jnp.full_like(s, coefs[-1])
    for c in coefs[-2::-1]:
        value = value * s + c
    return value


def turn(t):
    f = t - jnp.floor(t + 0.5)
    s = f * f
    c = poly(COS, s)
    n = f * poly(SIN, s)
    n2 = n + n
    return 1.0 - n2 * n, n2 * c


def gen_axis(first, rate, place, amp):
    lane = lax.broadcasted_iota(jnp.int32, (SLAB, BP), 0).astype(F32) + float(first)
    m = jnp.abs(lane - place) - HB
    re, im = turn(rate * (m * m))
    if amp is not None:
        re, im = amp[0] * re - amp[1] * im, amp[0] * im + amp[1] * re
    return lane, re, im


def fill(dst, tiles, col, params, sign_rows):
    rate, pos, amp = params
    k = jnp.floor(pos * (1.0 / T))
    place = pos - k * T
    count = len(tiles)
    need_hi = [(k == j).astype(F32).astype(BF) for j in tiles]
    need_lo = [(k == j - 1).astype(F32).astype(BF) for j in tiles]
    for first in range(0, T, SLAB):
        lane, re, im = gen_axis(first, rate, place, amp)
        above = lane >= place
        below = lane <= place
        hi_re = jnp.where(above, re, 0.0).astype(BF)
        hi_im = jnp.where(above, im, 0.0).astype(BF)
        lo_re = jnp.where(below, re, 0.0).astype(BF)
        lo_im = jnp.where(below, im, 0.0).astype(BF)
        for n, j in enumerate(tiles):
            if j == 0:
                t_re, t_im = hi_re * need_hi[n], hi_im * need_hi[n]
            else:
                t_re = hi_re * need_hi[n] + lo_re * need_lo[n]
                t_im = hi_im * need_hi[n] + lo_im * need_lo[n]
            row = n * T + first
            if sign_rows:
                im_row = count * T + row
                dst[row : row + SLAB, col : col + BP] = t_re
                dst[row : row + SLAB, col + BP : col + 2 * BP] = -t_im
                dst[im_row : im_row + SLAB, col : col + BP] = t_im
                dst[im_row : im_row + SLAB, col + BP : col + 2 * BP] = t_re
            else:
                dst[row : row + SLAB, col : col + BP] = t_re
                dst[row : row + SLAB, col + BP : col + 2 * BP] = t_im


def compact(near, packed, spans):
    total = near.shape[2]
    lane = lax.broadcasted_iota(jnp.int32, (len(SHIFTS), total), 1)
    which = lax.broadcasted_iota(jnp.int32, (len(SHIFTS), total), 0)

    def bound(pick):
        value = jnp.zeros((len(SHIFTS), total), F32)
        for i, span in enumerate(spans):
            value = jnp.where(which == i, float(span[pick]), value)
        return value

    data = [near[:, f, :] for f in range(5)]
    keep = lane.astype(F32) < near[:, 5, :] * float(BP)
    keep = keep & (data[0] >= bound(0)) & (data[0] < bound(1))
    keep = keep & (data[1] >= bound(2)) & (data[1] < bound(3))
    flag = keep.astype(F32)
    numbers = [jnp.sum(flag[i : i + 1]).astype(jnp.int32) for i in range(len(SHIFTS))]
    gaps = jnp.where(keep, 0, 1)
    step = 1
    while step < total:
        gaps = gaps + jnp.where(lane >= step, pltpu.roll(gaps, step, 1), 0)
        step *= 2
    move = jnp.where(keep, gaps, 0)
    data = [jnp.where(keep, d, 0.0) for d in data]
    step = 1
    while step < total:
        come = pltpu.roll(move, total - step, 1)
        arrives = (come & step) != 0
        leaves = (move & step) != 0
        move = jnp.where(arrives, come, jnp.where(leaves, 0, move))
        data = [
            jnp.where(arrives, pltpu.roll(d, total - step, 1), jnp.where(leaves, 0.0, d))
            for d in data
        ]
        step *= 2
    for f in range(5):
        packed[f] = data[f]
    return numbers


def add_source(pts, count, row_tiles, col_tiles, dst_row, dst_col, chunk, left, right, acc):
    nr, nc = len(row_tiles), len(col_tiles)

    @pl.loop(0, (count + chunk - 1) // chunk)
    def _(step):
        for b in range(chunk):
            offset = pl.multiple_of((step * chunk + b) * BP, BP)
            x = pts(0, offset)
            y = pts(1, offset)
            rate = pts(2, offset) * (0.5 / math.pi)
            amp = (pts(3, offset), pts(4, offset))
            fill(left, row_tiles, 2 * BP * b, (rate, y, None), True)
            fill(right, col_tiles, 2 * BP * b, (rate, x, amp), False)
        product = lax.dot_general(
            left[: 2 * nr * T, : 2 * BP * chunk],
            right[: nc * T, : 2 * BP * chunk],
            (((1,), (1,)), ((), ())),
            preferred_element_type=F32,
        )
        rows = slice(dst_row * T, (dst_row + nr) * T)
        cols = slice(dst_col * T, (dst_col + nc) * T)
        acc[0, rows, cols] += product[: nr * T]
        acc[1, rows, cols] += product[nr * T :]


def band(prop, in_dim):
    shape = (2 * T, T) if in_dim == 0 else (T, 2 * T)
    offset = (
        lax.broadcasted_iota(jnp.int32, shape, in_dim)
        - lax.broadcasted_iota(jnp.int32, shape, 1 - in_dim)
        - HB
    ).astype(F32)
    re, im = turn(prop * (0.5 / math.pi) * (offset * offset))
    inside = jnp.abs(offset) <= HB
    scale = 1.0 / math.sqrt(2 * HB + 1)
    return jnp.where(inside, re * scale, 0.0), jnp.where(inside, im * scale, 0.0)


def field_kernel(prop, own, near, out, left, right, acc, across, packed):
    rows_n, cols_n = acc.shape[1] // T, acc.shape[2] // T
    acc[...] = jnp.zeros_like(acc)
    all_rows, all_cols = list(range(rows_n)), list(range(cols_n))
    wide, high = float((cols_n - 1) * T), float((rows_n - 1) * T)
    reach_c = {-1: (wide - T, wide), 0: (0.0, wide), 1: (0.0, float(T))}
    reach_r = {-1: (high - T, high), 0: (0.0, high), 1: (0.0, float(T))}
    numbers = compact(near, packed, [reach_c[dx] + reach_r[dy] for dy, dx in SHIFTS])

    def own_points(f, offset):
        return own[f : f + 1, pl.ds(offset, BP)]

    count = jnp.max(own[5:6, :BP]).astype(jnp.int32)
    add_source(own_points, count, all_rows, all_cols, 0, 0, 4, left, right, acc)
    pick_r = {-1: ([rows_n - 1], 0), 0: (all_rows, 0), 1: ([0], rows_n - 1)}
    pick_c = {-1: ([cols_n - 1], 0), 0: (all_cols, 0), 1: ([0], cols_n - 1)}
    for index, (dy, dx) in enumerate(SHIFTS):
        (row_tiles, dst_row), (col_tiles, dst_col) = pick_r[dy], pick_c[dx]

        def points(f, offset):
            return packed[f, index : index + 1, pl.ds(offset, BP)]

        blocks = (numbers[index] + BP - 1) // BP
        add_source(points, blocks, row_tiles, col_tiles, dst_row, dst_col, 2 if dx == 0 else 1, left, right, acc)

    _, at_row, n_row, at_col, n_col = position()
    edges = (at_row == 0, at_row == n_row - 1, at_col == 0, at_col == n_col - 1)
    ends = (
        (slice(0, HB), slice(None)),
        (slice(rows_n * T - HB, rows_n * T), slice(None)),
    )
    for e, (r, c) in enumerate(ends):

        @pl.when(edges[e])
        def _():
            acc[:, r, c] = jnp.zeros_like(acc[:, r, c])

    lanes = lax.broadcasted_iota(jnp.int32, (1, T), 1)
    for e, col, keep in ((2, 0, lanes >= HB), (3, (cols_n - 1) * T, lanes < T - HB)):

        @pl.when(edges[e])
        def _():
            acc[:, :, col : col + T] = jnp.where(keep[None], acc[:, :, col : col + T], 0.0)

    re, im = band(prop[0], 0)
    table = jnp.concatenate(
        [jnp.concatenate([re, im], 1), jnp.concatenate([-im, re], 1)], 0
    )
    table = table.astype(BF)
    for j in range(cols_n - 1):
        cols = slice(j * T, (j + 2) * T)
        data = jnp.concatenate([acc[0, :, cols], acc[1, :, cols]], 1).astype(BF)
        result = jnp.dot(data, table, preferred_element_type=F32)
        across[0, :, j * T : (j + 1) * T] = result[:, :T].astype(BF)
        across[1, :, j * T : (j + 1) * T] = result[:, T:].astype(BF)

    re, im = band(prop[0], 1)
    table = jnp.concatenate(
        [jnp.concatenate([re, -im], 1), jnp.concatenate([im, re], 1)], 0
    )
    table = table.astype(BF)
    for q in range(rows_n - 1):
        rows = slice(q * T, (q + 2) * T)
        data = jnp.concatenate([across[0, rows, :], across[1, rows, :]], 0)
        result = jnp.dot(table, data, preferred_element_type=F32)
        out[0, q * T : (q + 1) * T, :] = result[:T]
        out[1, q * T : (q + 1) * T, :] = result[T:]


SHIFTS = ((0, -1), (0, 1), (-1, 0), (1, 0), (-1, -1), (-1, 1), (1, -1), (1, 1))


def position():
    n_sub = lax.axis_size("sub")
    at_row = lax.axis_index("row") * n_sub + lax.axis_index("sub")
    return n_sub, at_row, lax.axis_size("row") * n_sub, lax.axis_index("col"), lax.axis_size("col")


def exchange_kernel(counts, px, py, pr, pa, own_out, near_out, own, near, send, recv):
    n_sub, at_row, n_row, at_col, n_col = position()

    def neighbour(dy, dx):
        y, x = at_row + dy, at_col + dx
        there = (y >= 0) & (y < n_row) & (x >= 0) & (x < n_col)
        return there, (lax.axis_index("grp"), x, lax.div(y, n_sub), lax.rem(y, n_sub))

    barrier = pltpu.get_barrier_semaphore()
    for shift in SHIFTS:
        there, device = neighbour(*shift)

        @pl.when(there)
        def _():
            pl.semaphore_signal(
                barrier, inc=1, device_id=device, device_id_type=pl.DeviceIdType.MESH
            )

    count = counts[0, 0]
    live = lax.broadcasted_iota(jnp.int32, px.shape, 1) < count * BP
    own[0:1] = px[...].astype(F32)
    own[1:2] = py[...].astype(F32)
    own[2:3] = pr[...]
    own[3:4] = jnp.where(live, pa[0:1], 0.0)
    own[4:5] = jnp.where(live, pa[1:2], 0.0)
    own[5:8] = jnp.broadcast_to(count.astype(F32), (3, px.shape[1]))
    own_out[...] = own[...]

    tall = 3 - (at_row == 0).astype(jnp.int32) - (at_row == n_row - 1).astype(jnp.int32)
    broad = 3 - (at_col == 0).astype(jnp.int32) - (at_col == n_col - 1).astype(jnp.int32)
    pl.semaphore_wait(barrier, tall * broad - 1)

    def copy(index, shift):
        there, device = neighbour(*shift)
        return there, pltpu.make_async_remote_copy(
            src_ref=own,
            dst_ref=near.at[index],
            send_sem=send.at[index],
            recv_sem=recv.at[index],
            device_id=device,
            device_id_type=pl.DeviceIdType.MESH,
        )

    back = [SHIFTS.index((-dy, -dx)) for dy, dx in SHIFTS]
    for index, shift in enumerate(SHIFTS):
        there, there_copy = copy(back[index], shift)

        @pl.when(there)
        def _():
            there_copy.start()

    for index, shift in enumerate(SHIFTS):
        there, _ = neighbour(*shift)
        _, incoming = copy(index, shift)

        @pl.when(there)
        def _():
            incoming.wait_recv()
            near_out[index] = near[index]

        @pl.when(jnp.logical_not(there))
        def _():
            near_out[index] = jnp.zeros_like(near_out[index])

    for index, shift in enumerate(SHIFTS):
        there, there_copy = copy(back[index], shift)

        @pl.when(there)
        def _():
            there_copy.wait_send()


def on_device(th, tw, counts, point_x, point_y, point_rate, point_amp, prop_rate):
    points = point_x.shape[-1]
    vmem = pl.BlockSpec(memory_space=pltpu.VMEM)
    smem = pl.BlockSpec(memory_space=pltpu.SMEM)
    own, near = pl.pallas_call(
        exchange_kernel,
        out_shape=[
            jax.ShapeDtypeStruct((FIELDS, points), F32),
            jax.ShapeDtypeStruct((len(SHIFTS), FIELDS, points), F32),
        ],
        in_specs=[smem, vmem, vmem, vmem, vmem],
        out_specs=[vmem, vmem],
        scratch_shapes=[
            pltpu.VMEM((FIELDS, points), F32),
            pltpu.VMEM((len(SHIFTS), FIELDS, points), F32),
            pltpu.SemaphoreType.DMA((len(SHIFTS),)),
            pltpu.SemaphoreType.DMA((len(SHIFTS),)),
        ],
        compiler_params=pltpu.CompilerParams(collective_id=0, has_side_effects=True),
    )(counts, point_x[0], point_y[0], point_rate[0], point_amp[0, 0])
    wide, high = tw + 2 * HB, th + 2 * HB
    return pl.pallas_call(
        field_kernel,
        out_shape=jax.ShapeDtypeStruct((2, th, tw), F32),
        in_specs=[smem, vmem, vmem],
        out_specs=vmem,
        scratch_shapes=[
            pltpu.VMEM((2 * high, 8 * BP), BF),
            pltpu.VMEM((wide, 8 * BP), BF),
            pltpu.VMEM((2, high, wide), F32),
            pltpu.VMEM((2, high, tw), BF),
            pltpu.VMEM((5, len(SHIFTS), points), F32),
        ],
        compiler_params=pltpu.CompilerParams(vmem_limit_bytes=48 * 1024 * 1024),
    )(prop_rate, own, near)


def solution(mesh):
    th, tw = 256, 512
    return jax.shard_map(
        functools.partial(on_device, th, tw),
        mesh=mesh,
        in_specs=(
            P(("grp", "row", "sub"), "col"),
            P(("grp", "row", "sub"), "col", None),
            P(("grp", "row", "sub"), "col", None),
            P(("grp", "row", "sub"), "col", None),
            P(("grp", "row", "sub"), "col", None, None),
            P(),
        ),
        out_specs=P(None, ("grp", "row", "sub"), "col"),
        check_vma=False,
    )
```

```python
import functools
import math

import jax
import jax.numpy as jnp
from jax import lax
from jax.experimental import pallas as pl
from jax.experimental.pallas import tpu as pltpu
from jax.sharding import PartitionSpec as P

HB = 64
BP = 128
T = 128
SLAB = 32
FIELDS = 8
BF = jnp.bfloat16
F32 = jnp.float32


def fitted(func, degree):
    import numpy as np

    nodes = 0.125 - 0.125 * np.cos(np.pi * (np.arange(64) + 0.5) / 64)
    return [float(v) for v in np.polynomial.Polynomial.fit(nodes, func(nodes), degree).convert().coef]


def cos_values(s):
    import numpy as np

    return np.cos(np.pi * np.sqrt(s))


def sin_values(s):
    import numpy as np

    return np.sinc(np.sqrt(s)) * np.pi


COS = fitted(cos_values, 3)
SIN = fitted(sin_values, 3)


def poly(coefs, s):
    value = jnp.full_like(s, coefs[-1])
    for c in coefs[-2::-1]:
        value = value * s + c
    return value


def turn(t):
    f = t - jnp.floor(t + 0.5)
    s = f * f
    c = poly(COS, s)
    n = f * poly(SIN, s)
    n2 = n + n
    return 1.0 - n2 * n, n2 * c


def gen_axis(first, rate, place, amp):
    lane = lax.broadcasted_iota(jnp.int32, (SLAB, BP), 0).astype(F32) + float(first)
    m = jnp.abs(lane - place) - HB
    re, im = turn(rate * (m * m))
    if amp is not None:
        re, im = amp[0] * re - amp[1] * im, amp[0] * im + amp[1] * re
    return lane, re, im


def fill(dst, tiles, col, params, sign_rows):
    rate, pos, amp = params
    k = jnp.floor(pos * (1.0 / T))
    place = pos - k * T
    count = len(tiles)
    need_hi = [(k == j).astype(F32).astype(BF) for j in tiles]
    need_lo = [(k == j - 1).astype(F32).astype(BF) for j in tiles]
    for first in range(0, T, SLAB):
        lane, re, im = gen_axis(first, rate, place, amp)
        above = lane >= place
        below = lane <= place
        hi_re = jnp.where(above, re, 0.0).astype(BF)
        hi_im = jnp.where(above, im, 0.0).astype(BF)
        lo_re = jnp.where(below, re, 0.0).astype(BF)
        lo_im = jnp.where(below, im, 0.0).astype(BF)
        for n, j in enumerate(tiles):
            if j == 0:
                t_re, t_im = hi_re * need_hi[n], hi_im * need_hi[n]
            else:
                t_re = hi_re * need_hi[n] + lo_re * need_lo[n]
                t_im = hi_im * need_hi[n] + lo_im * need_lo[n]
            row = n * T + first
            if sign_rows:
                im_row = count * T + row
                dst[row : row + SLAB, col : col + BP] = t_re
                dst[row : row + SLAB, col + BP : col + 2 * BP] = -t_im
                dst[im_row : im_row + SLAB, col : col + BP] = t_im
                dst[im_row : im_row + SLAB, col + BP : col + 2 * BP] = t_re
            else:
                dst[row : row + SLAB, col : col + BP] = t_re
                dst[row : row + SLAB, col + BP : col + 2 * BP] = t_im


def compact(near, packed, spans):
    total = near.shape[2]
    lane = lax.broadcasted_iota(jnp.int32, (len(SHIFTS), total), 1)
    which = lax.broadcasted_iota(jnp.int32, (len(SHIFTS), total), 0)

    def bound(pick):
        value = jnp.zeros((len(SHIFTS), total), F32)
        for i, span in enumerate(spans):
            value = jnp.where(which == i, float(span[pick]), value)
        return value

    data = [near[:, f, :] for f in range(5)]
    keep = lane.astype(F32) < near[:, 5, :] * float(BP)
    keep = keep & (data[0] >= bound(0)) & (data[0] < bound(1))
    keep = keep & (data[1] >= bound(2)) & (data[1] < bound(3))
    flag = keep.astype(F32)
    numbers = [jnp.sum(flag[i : i + 1]).astype(jnp.int32) for i in range(len(SHIFTS))]
    gaps = jnp.where(keep, 0, 1)
    step = 1
    while step < total:
        gaps = gaps + jnp.where(lane >= step, pltpu.roll(gaps, step, 1), 0)
        step *= 2
    move = jnp.where(keep, gaps, 0)
    data = [jnp.where(keep, d, 0.0) for d in data]
    step = 1
    while step < total:
        come = pltpu.roll(move, total - step, 1)
        arrives = (come & step) != 0
        leaves = (move & step) != 0
        move = jnp.where(arrives, come, jnp.where(leaves, 0, move))
        data = [
            jnp.where(arrives, pltpu.roll(d, total - step, 1), jnp.where(leaves, 0.0, d))
            for d in data
        ]
        step *= 2
    for f in range(5):
        packed[f] = data[f]
    return numbers


def add_source(pts, count, row_tiles, col_tiles, dst_row, dst_col, chunk, left, right, acc):
    nr, nc = len(row_tiles), len(col_tiles)

    @pl.loop(0, (count + chunk - 1) // chunk)
    def _(step):
        for b in range(chunk):
            offset = pl.multiple_of((step * chunk + b) * BP, BP)
            x = pts(0, offset)
            y = pts(1, offset)
            rate = pts(2, offset) * (0.5 / math.pi)
            amp = (pts(3, offset), pts(4, offset))
            fill(left, row_tiles, 2 * BP * b, (rate, y, None), True)
            fill(right, col_tiles, 2 * BP * b, (rate, x, amp), False)
        product = lax.dot_general(
            left[: 2 * nr * T, : 2 * BP * chunk],
            right[: nc * T, : 2 * BP * chunk],
            (((1,), (1,)), ((), ())),
            preferred_element_type=F32,
        )
        rows = slice(dst_row * T, (dst_row + nr) * T)
        cols = slice(dst_col * T, (dst_col + nc) * T)
        acc[0, rows, cols] += product[: nr * T]
        acc[1, rows, cols] += product[nr * T :]


def band(prop, in_dim):
    shape = (2 * T, T) if in_dim == 0 else (T, 2 * T)
    offset = (
        lax.broadcasted_iota(jnp.int32, shape, in_dim)
        - lax.broadcasted_iota(jnp.int32, shape, 1 - in_dim)
        - HB
    ).astype(F32)
    re, im = turn(prop * (0.5 / math.pi) * (offset * offset))
    inside = jnp.abs(offset) <= HB
    scale = 1.0 / math.sqrt(2 * HB + 1)
    return jnp.where(inside, re * scale, 0.0), jnp.where(inside, im * scale, 0.0)


def field_kernel(prop, own, near, out, left, right, acc, across, packed):
    rows_n, cols_n = acc.shape[1] // T, acc.shape[2] // T
    acc[...] = jnp.zeros_like(acc)
    all_rows, all_cols = list(range(rows_n)), list(range(cols_n))
    wide, high = float((cols_n - 1) * T), float((rows_n - 1) * T)
    reach_c = {-1: (wide - T, wide), 0: (0.0, wide), 1: (0.0, float(T))}
    reach_r = {-1: (high - T, high), 0: (0.0, high), 1: (0.0, float(T))}
    numbers = compact(near, packed, [reach_c[dx] + reach_r[dy] for dy, dx in SHIFTS])

    def own_points(f, offset):
        return own[f : f + 1, pl.ds(offset, BP)]

    count = jnp.max(own[5:6, :BP]).astype(jnp.int32)
    add_source(own_points, count, all_rows, all_cols, 0, 0, 6, left, right, acc)
    pick_r = {-1: ([rows_n - 1], 0), 0: (all_rows, 0), 1: ([0], rows_n - 1)}
    pick_c = {-1: ([cols_n - 1], 0), 0: (all_cols, 0), 1: ([0], cols_n - 1)}
    for index, (dy, dx) in enumerate(SHIFTS):
        (row_tiles, dst_row), (col_tiles, dst_col) = pick_r[dy], pick_c[dx]

        def points(f, offset):
            return packed[f, index : index + 1, pl.ds(offset, BP)]

        blocks = (numbers[index] + BP - 1) // BP
        add_source(points, blocks, row_tiles, col_tiles, dst_row, dst_col, 2 if dx == 0 else 1, left, right, acc)

    _, at_row, n_row, at_col, n_col = position()
    edges = (at_row == 0, at_row == n_row - 1, at_col == 0, at_col == n_col - 1)
    ends = (
        (slice(0, HB), slice(None)),
        (slice(rows_n * T - HB, rows_n * T), slice(None)),
    )
    for e, (r, c) in enumerate(ends):

        @pl.when(edges[e])
        def _():
            acc[:, r, c] = jnp.zeros_like(acc[:, r, c])

    lanes = lax.broadcasted_iota(jnp.int32, (1, T), 1)
    for e, col, keep in ((2, 0, lanes >= HB), (3, (cols_n - 1) * T, lanes < T - HB)):

        @pl.when(edges[e])
        def _():
            acc[:, :, col : col + T] = jnp.where(keep[None], acc[:, :, col : col + T], 0.0)

    re, im = band(prop[0], 0)
    table = jnp.concatenate(
        [jnp.concatenate([re, im], 1), jnp.concatenate([-im, re], 1)], 0
    )
    table = table.astype(BF)
    for j in range(cols_n - 1):
        cols = slice(j * T, (j + 2) * T)
        data = jnp.concatenate([acc[0, :, cols], acc[1, :, cols]], 1).astype(BF)
        result = jnp.dot(data, table, preferred_element_type=F32)
        across[0, :, j * T : (j + 1) * T] = result[:, :T].astype(BF)
        across[1, :, j * T : (j + 1) * T] = result[:, T:].astype(BF)

    re, im = band(prop[0], 1)
    table = jnp.concatenate(
        [jnp.concatenate([re, -im], 1), jnp.concatenate([im, re], 1)], 0
    )
    table = table.astype(BF)
    for q in range(rows_n - 1):
        rows = slice(q * T, (q + 2) * T)
        data = jnp.concatenate([across[0, rows, :], across[1, rows, :]], 0)
        result = jnp.dot(table, data, preferred_element_type=F32)
        out[0, q * T : (q + 1) * T, :] = result[:T]
        out[1, q * T : (q + 1) * T, :] = result[T:]


SHIFTS = ((0, -1), (0, 1), (-1, 0), (1, 0), (-1, -1), (-1, 1), (1, -1), (1, 1))


def position():
    n_sub = lax.axis_size("sub")
    at_row = lax.axis_index("row") * n_sub + lax.axis_index("sub")
    return n_sub, at_row, lax.axis_size("row") * n_sub, lax.axis_index("col"), lax.axis_size("col")


def exchange_kernel(counts, px, py, pr, pa, own_out, near_out, own, near, send, recv):
    n_sub, at_row, n_row, at_col, n_col = position()

    def neighbour(dy, dx):
        y, x = at_row + dy, at_col + dx
        there = (y >= 0) & (y < n_row) & (x >= 0) & (x < n_col)
        return there, (lax.axis_index("grp"), x, lax.div(y, n_sub), lax.rem(y, n_sub))

    barrier = pltpu.get_barrier_semaphore()
    for shift in SHIFTS:
        there, device = neighbour(*shift)

        @pl.when(there)
        def _():
            pl.semaphore_signal(
                barrier, inc=1, device_id=device, device_id_type=pl.DeviceIdType.MESH
            )

    count = counts[0, 0]
    live = lax.broadcasted_iota(jnp.int32, px.shape, 1) < count * BP
    own[0:1] = px[...].astype(F32)
    own[1:2] = py[...].astype(F32)
    own[2:3] = pr[...]
    own[3:4] = jnp.where(live, pa[0:1], 0.0)
    own[4:5] = jnp.where(live, pa[1:2], 0.0)
    own[5:8] = jnp.broadcast_to(count.astype(F32), (3, px.shape[1]))
    own_out[...] = own[...]

    tall = 3 - (at_row == 0).astype(jnp.int32) - (at_row == n_row - 1).astype(jnp.int32)
    broad = 3 - (at_col == 0).astype(jnp.int32) - (at_col == n_col - 1).astype(jnp.int32)
    pl.semaphore_wait(barrier, tall * broad - 1)

    def copy(index, shift):
        there, device = neighbour(*shift)
        return there, pltpu.make_async_remote_copy(
            src_ref=own,
            dst_ref=near.at[index],
            send_sem=send.at[index],
            recv_sem=recv.at[index],
            device_id=device,
            device_id_type=pl.DeviceIdType.MESH,
        )

    back = [SHIFTS.index((-dy, -dx)) for dy, dx in SHIFTS]
    for index, shift in enumerate(SHIFTS):
        there, there_copy = copy(back[index], shift)

        @pl.when(there)
        def _():
            there_copy.start()

    for index, shift in enumerate(SHIFTS):
        there, _ = neighbour(*shift)
        _, incoming = copy(index, shift)

        @pl.when(there)
        def _():
            incoming.wait_recv()
            near_out[index] = near[index]

        @pl.when(jnp.logical_not(there))
        def _():
            near_out[index] = jnp.zeros_like(near_out[index])

    for index, shift in enumerate(SHIFTS):
        there, there_copy = copy(back[index], shift)

        @pl.when(there)
        def _():
            there_copy.wait_send()


def on_device(th, tw, counts, point_x, point_y, point_rate, point_amp, prop_rate):
    points = point_x.shape[-1]
    vmem = pl.BlockSpec(memory_space=pltpu.VMEM)
    smem = pl.BlockSpec(memory_space=pltpu.SMEM)
    own, near = pl.pallas_call(
        exchange_kernel,
        out_shape=[
            jax.ShapeDtypeStruct((FIELDS, points), F32),
            jax.ShapeDtypeStruct((len(SHIFTS), FIELDS, points), F32),
        ],
        in_specs=[smem, vmem, vmem, vmem, vmem],
        out_specs=[vmem, vmem],
        scratch_shapes=[
            pltpu.VMEM((FIELDS, points), F32),
            pltpu.VMEM((len(SHIFTS), FIELDS, points), F32),
            pltpu.SemaphoreType.DMA((len(SHIFTS),)),
            pltpu.SemaphoreType.DMA((len(SHIFTS),)),
        ],
        compiler_params=pltpu.CompilerParams(collective_id=0, has_side_effects=True),
    )(counts, point_x[0], point_y[0], point_rate[0], point_amp[0, 0])
    wide, high = tw + 2 * HB, th + 2 * HB
    return pl.pallas_call(
        field_kernel,
        out_shape=jax.ShapeDtypeStruct((2, th, tw), F32),
        in_specs=[smem, vmem, vmem],
        out_specs=vmem,
        scratch_shapes=[
            pltpu.VMEM((2 * high, 12 * BP), BF),
            pltpu.VMEM((wide, 12 * BP), BF),
            pltpu.VMEM((2, high, wide), F32),
            pltpu.VMEM((2, high, tw), BF),
            pltpu.VMEM((5, len(SHIFTS), points), F32),
        ],
        compiler_params=pltpu.CompilerParams(vmem_limit_bytes=48 * 1024 * 1024),
    )(prop_rate, own, near)


def solution(mesh):
    th, tw = 256, 512
    return jax.shard_map(
        functools.partial(on_device, th, tw),
        mesh=mesh,
        in_specs=(
            P(("grp", "row", "sub"), "col"),
            P(("grp", "row", "sub"), "col", None),
            P(("grp", "row", "sub"), "col", None),
            P(("grp", "row", "sub"), "col", None),
            P(("grp", "row", "sub"), "col", None, None),
            P(),
        ),
        out_specs=P(None, ("grp", "row", "sub"), "col"),
        check_vma=False,
    )
```
